512 devices in a mesh: ctx: 32 (over y_lo, z), exp: 16 (over x, y_hi, core).
Axes of the slice: x: 4, y: 8 (y_hi: 2, y_lo: 4; y = y_hi * 4 + y_lo), z: 8, core: 2. Of those that a mesh axis runs over, the one named last changes fastest.
Arguments:
- queries: bfloat16 [2048, 4096], P('ctx', 'exp'), may hold values from -256 to 256
- keys: bfloat16 [2048, 1024], P('ctx'), may hold values from -6 to 6
- values: bfloat16 [2048, 1024], P('ctx'), may hold values from -6 to 6
- residual: bfloat16 [2048, 4096], P('ctx', 'exp'), may hold values from -20 to 20
- gain: bfloat16 [4096], P('exp'), may hold values from 0.5 to 2
- expert_ids: int32 [2048, 2], replicated, may hold values from 0 to 7, all different within a row; in each aligned block of 64 rows (0 to 63, 64 to 127, ...) at most 24 rows name the same one
- gate_weights: float32 [2048, 2], P('ctx'), may hold values from 0.2 to 1
- w_gate: bfloat16 [16, 4096, 4096], P('exp', None, 'ctx'), may hold values from -0.09375 to 0.09375
- w_up: bfloat16 [16, 4096, 4096], P('exp', None, 'ctx'), may hold values from -0.09375 to 0.09375
- w_down: bfloat16 [16, 4096, 4096], P('exp', None, 'ctx'), may hold values from -0.0625 to 0.0625
Outputs:
- mixed: bfloat16 [2048, 4096], P('ctx', 'exp')
The draws below stay inside these ranges and needn't reach their ends.
Inputs may be any that keep to these rules, and one draw needn't show every extreme that they name: `expert_ids`: A token's 2 experts differ. In each aligned block of 64 tokens no expert is named by more than 24 tokens, a bound that some block reaches.
All inputs are finite; a program needn't handle non-finite values.
Results may differ from the reference program's by a relative error of at most 0.015.
Values may be sent and summed in bfloat16 or wider, within the bound.
No kernel may reach another device: no remote copies, remote signals or barrier semaphores. Data moves between devices by JAX's collectives and lax.ppermute only.
A program may use at most 64 MiB of HBM per device.

```python
import math
import jax
import jax.numpy as jnp
import numpy as np
from jax import lax

D = 4096
FF = 8192
HEADS = 32
KV_HEADS = 8
HEAD_DIM = 128
EXPERTS = 8
TOP = 2
SEQ_DEV = 64
CAP = 24
SPLIT = 2
LENGTH = 2048


def shared_keys(key):
    base = jax.random.normal(key, (LENGTH, KV_HEADS * HEAD_DIM), jnp.float32)
    return jnp.clip(base, -6.0, 6.0)


def draw_keys(key, part):
    base = shared_keys(key)
    return base.astype(jnp.bfloat16)


def draw_queries(key, part):
    key = jax.random.fold_in(key, 4)
    drawn = jnp.clip(jax.random.normal(key, (LENGTH, HEADS * HEAD_DIM), jnp.float32), -6.0, 6.0)
    return drawn.astype(jnp.bfloat16)


def draw_residual(key, part):
    key = jax.random.fold_in(key, 5)
    columns = 0.1 * 10.0 ** (jnp.arange(D, dtype=jnp.float32) / D)
    rows = 10.0 ** (jax.random.uniform(jax.random.fold_in(key, 1), (LENGTH, 1), jnp.float32) - 0.5)
    base = jnp.clip(jax.random.normal(jax.random.fold_in(key, 3), (LENGTH, D), jnp.float32), -6.0, 6.0)
    return (base * rows * columns[None, :]).astype(jnp.bfloat16)


def shard_levels(own_key, dims, shards, low, largest):
    factor_of, own = 1.0, jax.random.fold_in(own_key, 6)
    for position, shards_of in shards:
        heights = jnp.exp(jax.random.uniform(jax.random.fold_in(own, position), (shards_of,), jnp.float32, low / len(shards), largest / len(shards)))
        factor_of = factor_of * jnp.repeat(heights, dims[position] // shards_of).reshape([-1 if axis == position else 1 for axis in range(len(dims))])
    return factor_of


def assign_block(own_key, own, number, rows, amount, top, most, skew):
    sequence = jax.random.permutation(own_key, amount)
    crowded, usual = shares(amount, rows * top, most, skew, True), shares(amount, rows * top, most, skew, False)
    places = jnp.arange(amount)

    def named(lengths, rotation):
        used = int((lengths > 0).sum())
        fixed = max(1, used // 4)
        moved = fixed + (places - fixed + rotation * (used - fixed)) % max(1, amount - fixed)
        return jnp.zeros((amount,), jnp.int32).at[sequence[jnp.where(places < fixed, places, moved)]].set(jnp.asarray(lengths, jnp.int32))

    lengths = jnp.where(number % 4 == 0, named(crowded, number // 4), named(usual, number - number // 4 - 1))
    mixed = jax.random.permutation(jax.random.fold_in(own, 3), amount)
    giver, sink = mixed[0:amount // 2 * 2:2], mixed[1:amount // 2 * 2:2]
    margin = jnp.minimum(lengths[giver] - 1, most - lengths[sink]) // 2
    margin = jnp.where((giver == sequence[0]) | (sink == sequence[0]) | (lengths[sink] == 0), 0, jnp.maximum(margin, 0))
    moved = jax.random.randint(jax.random.fold_in(own, 4), (amount // 2,), 0, 1 << 20) % (margin + 1)
    lengths = lengths.at[giver].add(-moved).at[sink].add(moved)
    items = jnp.searchsorted(jnp.cumsum(lengths), jnp.arange(rows * top), side="right").astype(jnp.int32)
    listing = items.reshape(top, rows).T
    listing = listing[jax.random.permutation(jax.random.fold_in(own, 1), rows)]
    rotation = jax.random.randint(jax.random.fold_in(own, 2), (rows, 1), 0, top)
    return jnp.take_along_axis(listing, (jnp.arange(top)[None, :] + rotation) % top, axis=1)


def shares(number_of, total, reach, skew, full):
    weights = [(1 << 20) // math.isqrt(standing ** skew) + 1 for standing in range(1, number_of + 1)]
    largest = reach if full else min(reach, max(-(-total // number_of), total * weights[0] // sum(weights)))
    least = 1 if total - largest >= number_of - 1 else 0
    counts, surplus = [largest] + [least] * (number_of - 1), total - largest - least * (number_of - 1)
    while surplus > 0:
        movable = [i for i in range(1, number_of) if counts[i] < largest] or [i for i in range(1, number_of) if counts[i] < reach]
        whole, remaining = sum([weights[i] for i in movable]), surplus
        for i in movable:
            extra = min(reach - counts[i], max(1, remaining * weights[i] // whole), surplus)
            counts[i] = counts[i] + extra
            surplus = surplus - extra
    return np.array(counts)


def gaussian(key, shape, width, limit, shards=(), held_as=jnp.bfloat16):
    factor_of = shard_levels(key, shape, shards, -0.22, 0.18) if shards else 1.0
    drawn = jax.random.normal(key, shape, jnp.float32) * width * factor_of
    return jnp.minimum(jnp.maximum(drawn, -limit), limit).astype(held_as)


def setup_inputs(seed: int = 0) -> dict:
    splits = jax.random.split(jax.random.key(seed), 11)
    queries = draw_queries(jax.random.fold_in(splits[10], 71), 0)
    keys = draw_keys(jax.random.fold_in(splits[10], 71), 0)
    values = gaussian(splits[2], (LENGTH, KV_HEADS * HEAD_DIM), 1.0, 6.0, ((0, 32),))
    residual = draw_residual(jax.random.fold_in(splits[10], 71), 0)
    gain = jnp.clip(jnp.exp(math.log(2.0) - 1.3862944 * jax.random.uniform(splits[4], (D,), jnp.float32) ** shard_levels(splits[4], (D,), ((0, 16),), -0.2, 0.2)), 0.5, 2.0).astype(jnp.bfloat16)
    expert_ids_keys = jax.random.split(jax.random.fold_in(splits[5], 1), LENGTH // SEQ_DEV)
    expert_ids_turns = jax.random.permutation(jax.random.fold_in(splits[5], 3), LENGTH // SEQ_DEV)
    expert_ids = jax.vmap(lambda own, number: assign_block(jax.random.fold_in(splits[5], 2), own, number, SEQ_DEV, EXPERTS, TOP, CAP, 2))(expert_ids_keys, expert_ids_turns).reshape((LENGTH, TOP))
    gate_weights = jnp.clip(0.2 + 0.8 * jax.random.uniform(splits[6], (LENGTH, TOP), jnp.float32) ** shard_levels(splits[6], (LENGTH, TOP), ((0, 32),), -0.2, 0.2), 0.2, 1.0)
    w_gate = gaussian(splits[7], (EXPERTS * SPLIT, D, FF // SPLIT), D ** -0.5, 0.09375, ((0, 16), (2, 32)))
    w_up = gaussian(splits[8], (EXPERTS * SPLIT, D, FF // SPLIT), D ** -0.5, 0.09375, ((0, 16), (2, 32)))
    w_down = gaussian(splits[9], (EXPERTS * SPLIT, FF // SPLIT, D), FF ** -0.5, 0.0625, ((0, 16), (2, 32)))
    return dict(queries=queries, keys=keys, values=values, residual=residual, gain=gain, expert_ids=expert_ids, gate_weights=gate_weights, w_gate=w_gate, w_up=w_up, w_down=w_down)


epsilon = 1e-05
masked_score = -1e+30

def slot_numbers(routing):
    flat = routing.reshape(-1)
    hits = (flat[:, None] == jnp.arange(EXPERTS, dtype=jnp.int32)[None, :]).astype(jnp.int32)
    before = jnp.cumsum(hits, axis=0) - hits
    return lax.optimization_barrier(jnp.sum(before * hits, axis=1)).reshape(routing.shape)

def placement_table(routing, weights):
    slots = slot_numbers(routing)
    expert_hit = (routing[:, :, None] == jnp.arange(EXPERTS, dtype=jnp.int32)[None, None, :]).astype(jnp.float32)
    slot_hit = (slots[:, :, None] == jnp.arange(CAP, dtype=jnp.int32)[None, None, :]).astype(jnp.float32)
    return jnp.einsum('ske,skc,sk->ecs', expert_hit, slot_hit, weights.astype(jnp.float32), precision=lax.Precision.HIGHEST)

def attention(queries, keys, values):
    length = queries.shape[0]
    group = HEADS // KV_HEADS
    scale = 1.0 / math.sqrt(HEAD_DIM)
    positions = jnp.arange(length, dtype=jnp.int32)
    causal = positions[:, None] >= positions[None, :]
    query_heads = queries.reshape(length, HEADS, HEAD_DIM)
    key_heads = keys.reshape(length, KV_HEADS, HEAD_DIM)
    value_heads = values.reshape(length, KV_HEADS, HEAD_DIM)

    def one_head(head):
        query = query_heads[:, head]
        key_block = key_heads[:, head // group]
        value_block = value_heads[:, head // group]
        scores = jnp.dot(query, key_block.T, preferred_element_type=jnp.float32) * scale
        scores = jnp.where(causal, scores, masked_score)
        highest = lax.optimization_barrier(jnp.max(scores, axis=1, keepdims=True))
        weights = jnp.where(causal, jnp.exp(scores - highest), 0.0)
        total = lax.optimization_barrier(jnp.sum(weights, axis=1, keepdims=True))
        summed = jnp.dot(weights.astype(jnp.bfloat16), value_block, preferred_element_type=jnp.float32)
        return summed / total
    heads_out = lax.map(one_head, jnp.arange(HEADS, dtype=jnp.int32))
    return jnp.transpose(heads_out, (1, 0, 2)).reshape(length, HEADS * HEAD_DIM).astype(jnp.bfloat16)

def reference(queries, keys, values, residual, gain, expert_ids, gate_weights, w_gate, w_up, w_down):
    heads = attention(queries, keys, values)
    stream = (residual.astype(jnp.float32) + heads.astype(jnp.float32)).astype(jnp.bfloat16)
    stream_wide = stream.astype(jnp.float32)
    mean_square = lax.optimization_barrier(jnp.mean(stream_wide * stream_wide, axis=1, keepdims=True))
    normed = (stream_wide * lax.rsqrt(mean_square + epsilon) * gain.astype(jnp.float32)[None, :]).astype(jnp.bfloat16)
    blocks = LENGTH // SEQ_DEV
    normed_blocks = normed.reshape(blocks, SEQ_DEV, D).astype(jnp.float32)
    routing = expert_ids.reshape(blocks, SEQ_DEV, TOP)
    gates = gate_weights.reshape(blocks, SEQ_DEV, TOP)
    gather_table = jax.vmap(placement_table)(routing, jnp.ones_like(gates))
    combine_table = jax.vmap(placement_table)(routing, gates)
    rows = jnp.einsum('becs,bsd->ebcd', gather_table, normed_blocks, precision=lax.Precision.HIGHEST).astype(jnp.bfloat16)
    rows = rows.reshape(EXPERTS, blocks * CAP, D)

    def expert_part(index):
        taken = rows[index // SPLIT]
        gate = jnp.dot(taken, w_gate[index], preferred_element_type=jnp.float32)
        upper = jnp.dot(taken, w_up[index], preferred_element_type=jnp.float32)
        hidden = (jax.nn.silu(gate) * upper).astype(jnp.bfloat16)
        return jnp.dot(hidden, w_down[index], preferred_element_type=jnp.float32).astype(jnp.bfloat16)
    parts = lax.map(expert_part, jnp.arange(EXPERTS * SPLIT, dtype=jnp.int32))
    experts_out = lax.optimization_barrier(jnp.sum(parts.astype(jnp.float32).reshape(EXPERTS, SPLIT, blocks, CAP, D), axis=1))
    routed = jnp.einsum('becs,ebcd->bsd', combine_table, experts_out, precision=lax.Precision.HIGHEST)
    return (stream_wide + routed.reshape(blocks * SEQ_DEV, D)).astype(jnp.bfloat16)
```

```python
import math

import jax
import jax.numpy as jnp
from jax import lax
from jax.experimental import pallas as pl
from jax.experimental.pallas import tpu as pltpu
from jax.sharding import Mesh, PartitionSpec as P

D = 4096
HEADS = 32
KV_HEADS = 8
HEAD_DIM = 128
EXPERTS = 8
CAP = 24
HALF = CAP // 2
PAD = 16

epsilon = 1e-05
masked_score = -1e30

CTX = ("yp", "ya", "z")
EXP = ("x", "h", "k")
SWAP = [(0, 1), (1, 0)]


def swap(value, axis):
    return lax.ppermute(value, axis, SWAP)


def slot_rows(routing):
    tokens, top = routing.shape
    flat = routing.reshape(-1)
    hits = (flat[:, None] == jnp.arange(EXPERTS, dtype=jnp.int32)[None, :]).astype(jnp.bfloat16)
    count = tokens * top
    order = jnp.arange(count, dtype=jnp.int32)
    earlier = (order[:, None] > order[None, :]).astype(jnp.bfloat16)
    before = jnp.dot(earlier, hits, preferred_element_type=jnp.float32)
    slots = jnp.sum(before * hits.astype(jnp.float32), axis=1).astype(jnp.int32)
    rows = flat * (2 * PAD) + jnp.where(slots >= HALF, slots - HALF + PAD, slots)
    return rows.reshape(tokens, top)


def attention(queries, keys, values, first):
    rows = queries.shape[0]
    heads = queries.shape[1] // HEAD_DIM
    query = jnp.transpose(queries.reshape(rows, heads, HEAD_DIM), (1, 0, 2)).reshape(
        heads * rows, HEAD_DIM
    )
    scores = lax.dot_general(
        query, keys, (((1,), (1,)), ((), ())), preferred_element_type=jnp.float32
    ) * (1.0 / math.sqrt(HEAD_DIM))
    count = keys.shape[0]
    positions = first + jnp.arange(heads * rows, dtype=jnp.int32) % rows
    visible = positions[:, None] >= jnp.arange(count, dtype=jnp.int32)[None, :]
    scores = jnp.where(visible, scores, masked_score)
    highest = jnp.max(scores, axis=1, keepdims=True)
    weights = jnp.where(visible, jnp.exp(scores - highest), 0.0)
    total = jnp.sum(weights, axis=1, keepdims=True)
    summed = jnp.dot(weights.astype(jnp.bfloat16), values, preferred_element_type=jnp.float32)
    out = (summed / total).reshape(heads, rows, HEAD_DIM)
    return jnp.transpose(out, (1, 0, 2)).reshape(rows, heads * HEAD_DIM).astype(jnp.bfloat16)


def gate_up_kernel(place, rows, *refs):
    gates, uppers, out, total = refs[0:4], refs[4:8], refs[8], refs[9]
    step = pl.program_id(0)

    @pl.when(step == 0)
    def _():
        total[...] = jnp.zeros_like(total)

    weights = jnp.concatenate([ref[...] for ref in gates + uppers], axis=1)
    total[...] += jnp.dot(rows[...], weights, preferred_element_type=jnp.float32)

    @pl.when(step == pl.num_programs(0) - 1)
    def _():
        width = total.shape[1] // 2
        gate = total[:, :width]
        upper = total[:, width:]
        hidden = (gate / (1.0 + jnp.exp(-gate)) * upper).astype(jnp.bfloat16)
        first = place[1] == 0
        unit = width // 4
        for part in range(2):
            mine = hidden[:, 2 * part * unit : (2 * part + 1) * unit]
            other = hidden[:, (2 * part + 1) * unit : (2 * part + 2) * unit]
            out[:, 2 * part * unit : (2 * part + 1) * unit] = jnp.where(first, mine, other)
            out[:, (2 * part + 1) * unit : (2 * part + 2) * unit] = jnp.where(first, other, mine)


def gate_up(place, rows, gates, uppers):
    count, depth = rows.shape
    unit = gates[0].shape[1]
    chunk = 512
    return pl.pallas_call(
        gate_up_kernel,
        out_shape=jax.ShapeDtypeStruct((count, 4 * unit), jnp.bfloat16),
        grid_spec=pltpu.PrefetchScalarGridSpec(
            num_scalar_prefetch=1,
            grid=(depth // chunk,),
            in_specs=[pl.BlockSpec((count, chunk), lambda i, place: (0, i))]
            + [pl.BlockSpec((chunk, unit), lambda i, place: (i, 0))] * 8,
            out_specs=pl.BlockSpec((count, 4 * unit), lambda i, place: (0, 0)),
            scratch_shapes=[pltpu.VMEM((count, 8 * unit), jnp.float32)],
        ),
        compiler_params=pltpu.CompilerParams(vmem_limit_bytes=32 * 1024 * 1024),
        cost_estimate=pl.CostEstimate(
            flops=2 * count * depth * 8 * unit,
            bytes_accessed=2 * depth * (count + 8 * unit),
            transcendentals=count * 4 * unit,
        ),
    )(place, rows, *gates, *uppers)


def down_kernel(place, mine, other, *refs):
    weights, out = refs[0:4], refs[4]
    first = place[0] == 0
    unit = mine.shape[1] // 4
    total = None
    for part in range(2):
        own = mine[:, 2 * part * unit : (2 * part + 2) * unit]
        far = other[:, 2 * part * unit : (2 * part + 2) * unit]
        hidden = jnp.concatenate([jnp.where(first, own, far), jnp.where(first, far, own)], axis=1)
        columns = jnp.concatenate([weights[2 * part][0], weights[2 * part + 1][0]], axis=1)
        product = jnp.dot(hidden, columns, preferred_element_type=jnp.float32)
        total = product if total is None else total + product
    total = total.astype(jnp.bfloat16)
    width = total.shape[1] // 2
    out[place[1]] = total[:, :width]
    out[1 - place[1]] = total[:, width:]


def down(place, mine, other, weights):
    count = mine.shape[0]
    groups, depth, unit = weights[0].shape
    return pl.pallas_call(
        down_kernel,
        out_shape=jax.ShapeDtypeStruct((2, count, groups * unit), jnp.bfloat16),
        grid_spec=pltpu.PrefetchScalarGridSpec(
            num_scalar_prefetch=1,
            grid=(groups,),
            in_specs=[pl.BlockSpec(mine.shape, lambda i, place: (0, 0))] * 2
            + [pl.BlockSpec((1, depth, unit), lambda i, place: (i, 0, 0))] * 4,
            out_specs=pl.BlockSpec((2, count, unit), lambda i, place: (0, 0, i)),
        ),
        compiler_params=pltpu.CompilerParams(vmem_limit_bytes=32 * 1024 * 1024),
        cost_estimate=pl.CostEstimate(
            flops=2 * count * 2 * depth * 2 * groups * unit,
            bytes_accessed=2 * (2 * count * mine.shape[1] + 4 * groups * depth * unit),
            transcendentals=0,
        ),
    )(place, mine, other, *weights)


def shards(queries, keys, values, residual, gain, expert_ids, gate_weights, w_gate, w_up, w_down):
    seq_rows = queries.shape[0]
    width = queries.shape[1]
    z_count = lax.axis_size("z")
    ctx_count = lax.axis_size(CTX)
    exp_count = lax.axis_size(EXP)
    ctx_index = lax.axis_index(CTX)
    core = lax.axis_index("k")
    place = jnp.stack([lax.axis_index("yp"), lax.axis_index("ya")]).astype(jnp.int32)

    head = (lax.axis_index("x") * 2 + lax.axis_index("h")) * HEAD_DIM
    key_part = lax.dynamic_slice_in_dim(keys, head, HEAD_DIM, 1)
    value_part = lax.dynamic_slice_in_dim(values, head, HEAD_DIM, 1)
    sent = jnp.where(core == 0, key_part, value_part)
    held = lax.all_to_all(
        jnp.broadcast_to(sent[None], (ctx_count, seq_rows, HEAD_DIM)), CTX, 0, 0, tiled=True
    ).reshape(ctx_count * seq_rows, HEAD_DIM)
    far = swap(held, "k")
    all_keys = jnp.where(core == 0, held, far)
    all_values = jnp.where(core == 0, far, held)

    def four(own):
        side = swap(own, "ya")
        return [own, side, swap(own, "k"), swap(side, "k")]

    gates = four(w_gate[0])
    uppers = four(w_up[0])
    unit = w_down.shape[2]
    cut = w_down[0].reshape(ctx_count // z_count, z_count, unit, unit)
    cut = jnp.transpose(cut, (1, 0, 2, 3)).reshape(z_count, ctx_count // z_count * unit, unit)
    downs = four(lax.all_to_all(cut, "z", 0, 0, tiled=True))

    heads = attention(queries, all_keys, all_values, ctx_index * seq_rows)
    stream = (residual.astype(jnp.float32) + heads.astype(jnp.float32)).astype(jnp.bfloat16)

    block_ids = lax.dynamic_slice_in_dim(expert_ids, ctx_index * seq_rows, seq_rows, 0)
    rows_of = slot_rows(block_ids)
    table_rows = EXPERTS * 2 * PAD
    row_id = jnp.arange(table_rows, dtype=jnp.int32)
    taken = (row_id[:, None] == rows_of[None, :, 0]) | (row_id[:, None] == rows_of[None, :, 1])
    gain_row = ((row_id % PAD) == HALF)[:, None]
    table = jnp.concatenate(
        [taken, gain_row, jnp.zeros((table_rows, 15), jnp.bool_)], axis=1
    ).astype(jnp.bfloat16)
    source = jnp.concatenate(
        [stream, gain[None, :], jnp.zeros((15, width), jnp.bfloat16)], axis=0
    )
    outgoing = jnp.dot(table, source, preferred_element_type=jnp.float32).astype(jnp.bfloat16)
    outgoing = jnp.broadcast_to(
        outgoing.reshape(1, exp_count, PAD, width), (2, exp_count, PAD, width)
    ).reshape(2 * exp_count, PAD, width)
    arrived = lax.all_to_all(outgoing, ("yp",) + EXP, 0, 0, tiled=True)
    arrived = arrived.reshape(2, exp_count, PAD, width).astype(jnp.float32)
    rows = arrived[:, :, :HALF]
    all_gain = arrived[0, :, HALF]
    mean_square = jnp.sum(rows * rows, axis=(1, 3), keepdims=True) / D
    normed = (rows * lax.rsqrt(mean_square + epsilon) * all_gain[None, :, None, :]).astype(
        jnp.bfloat16
    )
    piece = jnp.transpose(normed, (0, 2, 1, 3)).reshape(CAP, exp_count * width)

    all_rows = lax.all_gather(piece, "z", axis=0, tiled=True)
    hidden = gate_up(place, all_rows, gates, uppers)
    out = down(place, hidden, swap(hidden, "yp"), downs)

    half_columns = out.shape[2]
    back = out.reshape(2, z_count, 2, HALF, half_columns)
    back = jnp.transpose(back, (2, 1, 0, 3, 4)).reshape(2 * z_count, 2, HALF, half_columns)
    back = lax.all_to_all(back, ("yp", "z"), 0, 0, tiled=True)
    back = back.reshape(2, z_count, 2, HALF, half_columns).astype(jnp.float32)
    summed = jnp.sum(back, axis=1).astype(jnp.bfloat16)
    summed = summed.reshape(4, HALF, half_columns // width, width)
    summed = jnp.transpose(summed, (0, 2, 1, 3)).reshape(exp_count, HALF, width)
    summed = jnp.pad(summed, ((0, 0), (0, PAD - HALF), (0, 0)))
    returned = lax.all_to_all(summed, EXP, 0, 0, tiled=True).reshape(table_rows, width)
    mix = jnp.where(rows_of[:, 0:1] == row_id[None, :], gate_weights[:, 0:1], 0.0) + jnp.where(
        rows_of[:, 1:2] == row_id[None, :], gate_weights[:, 1:2], 0.0
    )
    routed = jnp.dot(mix, returned.astype(jnp.float32), precision=lax.Precision.HIGHEST)
    return (stream.astype(jnp.float32) + routed).astype(jnp.bfloat16)


def solution(mesh):
    split = Mesh(
        mesh.devices.reshape(2, 2, 8, 4, 2, 2), ("yp", "ya", "z", "x", "h", "k")
    )
    return jax.shard_map(
        shards,
        mesh=split,
        in_specs=(
            P(CTX, EXP),
            P(CTX, None),
            P(CTX, None),
            P(CTX, EXP),
            P(EXP),
            P(),
            P(CTX, None),
            P(EXP, None, CTX),
            P(EXP, None, CTX),
            P(EXP, None, CTX),
        ),
        out_specs=P(CTX, EXP),
        check_vma=False,
    )
```

```python
import math

import jax
import jax.numpy as jnp
from jax import lax
from jax.experimental import pallas as pl
from jax.experimental.pallas import tpu as pltpu
from jax.sharding import Mesh, PartitionSpec as P

D = 4096
HEADS = 32
KV_HEADS = 8
HEAD_DIM = 128
EXPERTS = 8
CAP = 24
HALF = CAP // 2
PAD = 16

epsilon = 1e-05
masked_score = -1e30

CTX = ("yp", "ya", "z")
EXP = ("x", "h", "k")
SWAP = [(0, 1), (1, 0)]


def swap(value, axis):
    return lax.ppermute(value, axis, SWAP)


def slot_rows(routing):
    tokens, top = routing.shape
    flat = routing.reshape(-1)
    hits = (flat[:, None] == jnp.arange(EXPERTS, dtype=jnp.int32)[None, :]).astype(jnp.bfloat16)
    count = tokens * top
    order = jnp.arange(count, dtype=jnp.int32)
    earlier = (order[:, None] > order[None, :]).astype(jnp.bfloat16)
    before = jnp.dot(earlier, hits, preferred_element_type=jnp.float32)
    slots = jnp.sum(before * hits.astype(jnp.float32), axis=1).astype(jnp.int32)
    rows = flat * (2 * PAD) + jnp.where(slots >= HALF, slots - HALF + PAD, slots)
    return rows.reshape(tokens, top)


def attention(queries, keys, values, first):
    rows = queries.shape[0]
    heads = queries.shape[1] // HEAD_DIM
    query = jnp.transpose(queries.reshape(rows, heads, HEAD_DIM), (1, 0, 2)).reshape(
        heads * rows, HEAD_DIM
    )
    scores = lax.dot_general(
        query, keys, (((1,), (1,)), ((), ())), preferred_element_type=jnp.float32
    ) * (1.0 / math.sqrt(HEAD_DIM))
    count = keys.shape[0]
    positions = first + jnp.arange(heads * rows, dtype=jnp.int32) % rows
    visible = positions[:, None] >= jnp.arange(count, dtype=jnp.int32)[None, :]
    scores = jnp.where(visible, scores, masked_score)
    highest = jnp.max(scores, axis=1, keepdims=True)
    weights = jnp.where(visible, jnp.exp(scores - highest), 0.0)
    total = jnp.sum(weights, axis=1, keepdims=True)
    summed = jnp.dot(weights.astype(jnp.bfloat16), values, preferred_element_type=jnp.float32)
    out = (summed / total).reshape(heads, rows, HEAD_DIM)
    return jnp.transpose(out, (1, 0, 2)).reshape(rows, heads * HEAD_DIM).astype(jnp.bfloat16)


def gate_up_kernel(place, rows, gate_own, gate_far, *refs):
    uppers, out, total = refs[0:4], refs[4], refs[5]
    step = pl.program_id(0)
    columns = [gate_own[0], gate_own[1], gate_far[0], gate_far[1]] + [ref[...] for ref in uppers]
    product = jnp.dot(
        rows[...], jnp.concatenate(columns, axis=1), preferred_element_type=jnp.float32
    )

    @pl.when(step == 0)
    def _():
        total[...] = product

    @pl.when(step != 0)
    def _():
        total[...] += product

    @pl.when(step == pl.num_programs(0) - 1)
    def _():
        unit = gate_own.shape[2]
        first = place[1] == 0
        for part in range(2):
            mine = total[:, (4 + 2 * part) * unit : (5 + 2 * part) * unit]
            side = total[:, (5 + 2 * part) * unit : (6 + 2 * part) * unit]
            for half in range(2):
                at = 2 * part + half
                gate = total[:, at * unit : (at + 1) * unit]
                upper = jnp.where(first, mine, side) if half == 0 else jnp.where(first, side, mine)
                hidden = gate / (1.0 + jnp.exp(-gate)) * upper
                out[:, at * unit : (at + 1) * unit] = hidden.astype(jnp.bfloat16)


def gate_up(place, rows, gates, uppers):
    count, depth = rows.shape
    unit = uppers[0].shape[1]
    chunk = 1024
    return pl.pallas_call(
        gate_up_kernel,
        out_shape=jax.ShapeDtypeStruct((count, 4 * unit), jnp.bfloat16),
        grid_spec=pltpu.PrefetchScalarGridSpec(
            num_scalar_prefetch=1,
            grid=(depth // chunk,),
            in_specs=[pl.BlockSpec((count, chunk), lambda i, place: (0, i))]
            + [pl.BlockSpec((2, chunk, unit), lambda i, place: (0, i, 0))] * 2
            + [pl.BlockSpec((chunk, unit), lambda i, place: (i, 0))] * 4,
            out_specs=pl.BlockSpec((count, 4 * unit), lambda i, place: (0, 0)),
            scratch_shapes=[pltpu.VMEM((count, 8 * unit), jnp.float32)],
        ),
        compiler_params=pltpu.CompilerParams(vmem_limit_bytes=32 * 1024 * 1024),
        cost_estimate=pl.CostEstimate(
            flops=2 * count * depth * 8 * unit,
            bytes_accessed=2 * depth * (count + 8 * unit),
            transcendentals=count * 4 * unit,
        ),
    )(place, rows, *gates, *uppers)


def down_kernel(place, hidden, own, far, out):
    rows = hidden.shape[1]
    unit = hidden.shape[2] // 4
    first = place[0] == 0
    step = pl.program_id(0)
    for parity in range(2):
        pieces = []
        for part in range(2):
            for high in range(2):
                pieces.append(hidden[2 * high + parity, :, 2 * part * unit : (2 * part + 2) * unit])
        own_hidden = jnp.concatenate(pieces[0:2], axis=1)
        far_hidden = jnp.concatenate(pieces[2:4], axis=1)
        own_columns = jnp.concatenate([own[0], own[1]], axis=1)
        far_columns = jnp.concatenate([far[0], far[1]], axis=1)
        total = jnp.dot(own_hidden, own_columns, preferred_element_type=jnp.float32)
        total += jnp.dot(far_hidden, far_columns, preferred_element_type=jnp.float32)
        out[parity] = total.astype(jnp.bfloat16)


def down(place, hidden, own, far):
    count = hidden.shape[1]
    groups, depth, unit = own.shape
    return pl.pallas_call(
        down_kernel,
        out_shape=jax.ShapeDtypeStruct((2, count, groups * unit), jnp.bfloat16),
        grid_spec=pltpu.PrefetchScalarGridSpec(
            num_scalar_prefetch=1,
            grid=(groups // 2,),
            in_specs=[pl.BlockSpec(hidden.shape, lambda i, place: (0, 0, 0))]
            + [pl.BlockSpec((2, depth, unit), lambda i, place: (i, 0, 0))] * 2,
            out_specs=pl.BlockSpec((2, count, 2 * unit), lambda i, place: (0, 0, i)),
        ),
        compiler_params=pltpu.CompilerParams(vmem_limit_bytes=32 * 1024 * 1024),
        cost_estimate=pl.CostEstimate(
            flops=2 * 2 * count * 2 * depth * groups * unit,
            bytes_accessed=2 * (hidden.size + 2 * own.size + 2 * count * groups * unit),
            transcendentals=0,
        ),
    )(place, hidden, own, far)


def shards(queries, keys, values, residual, gain, expert_ids, gate_weights, w_gate, w_up, w_down):
    seq_rows = queries.shape[0]
    width = queries.shape[1]
    z_count = lax.axis_size("z")
    ctx_count = lax.axis_size(CTX)
    exp_count = lax.axis_size(EXP)
    ctx_index = lax.axis_index(CTX)
    core = lax.axis_index("k")
    place = jnp.stack([lax.axis_index("yp"), lax.axis_index("ya")]).astype(jnp.int32)

    head = (lax.axis_index("x") * 2 + lax.axis_index("h")) * HEAD_DIM
    key_part = lax.dynamic_slice_in_dim(keys, head, HEAD_DIM, 1)
    value_part = lax.dynamic_slice_in_dim(values, head, HEAD_DIM, 1)
    sent = jnp.where(core == 0, key_part, value_part)
    gate_own = lax.all_gather(w_gate[0], "ya")
    held = lax.all_to_all(
        jnp.broadcast_to(sent[None], (ctx_count, seq_rows, HEAD_DIM)), CTX, 0, 0, tiled=True
    ).reshape(ctx_count * seq_rows, HEAD_DIM)
    w_up, w_down, held = lax.optimization_barrier((w_up, w_down, held))
    up_side = swap(w_up[0], "ya")
    far = swap(held, "k")
    all_keys = jnp.where(core == 0, held, far)
    all_values = jnp.where(core == 0, far, held)

    unit = w_down.shape[2]
    cut = w_down[0].reshape(ctx_count // z_count, z_count, unit, unit)
    cut = jnp.transpose(cut, (1, 0, 2, 3)).reshape(z_count, ctx_count // z_count * unit, unit)
    down_own = lax.all_to_all(cut, "z", 0, 0, tiled=True)

    heads = attention(queries, all_keys, all_values, ctx_index * seq_rows)
    stream = (residual.astype(jnp.float32) + heads.astype(jnp.float32)).astype(jnp.bfloat16)

    block_ids = lax.dynamic_slice_in_dim(expert_ids, ctx_index * seq_rows, seq_rows, 0)
    rows_of = slot_rows(block_ids)
    table_rows = EXPERTS * 2 * PAD
    row_id = jnp.arange(table_rows, dtype=jnp.int32)
    taken = (row_id[:, None] == rows_of[None, :, 0]) | (row_id[:, None] == rows_of[None, :, 1])
    gain_row = ((row_id % PAD) == HALF)[:, None]
    table = jnp.concatenate(
        [taken, gain_row, jnp.zeros((table_rows, 15), jnp.bool_)], axis=1
    ).astype(jnp.bfloat16)
    source = jnp.concatenate(
        [stream, gain[None, :], jnp.zeros((15, width), jnp.bfloat16)], axis=0
    )
    outgoing = jnp.dot(table, source, preferred_element_type=jnp.float32).astype(jnp.bfloat16)
    outgoing = jnp.broadcast_to(
        outgoing.reshape(1, exp_count, PAD, width), (2, exp_count, PAD, width)
    ).reshape(2 * exp_count, PAD, width)
    arrived = lax.all_to_all(outgoing, ("yp",) + EXP, 0, 0, tiled=True)
    arrived = arrived.reshape(2, exp_count, PAD, width).astype(jnp.float32)
    rows = arrived[:, :, :HALF]
    all_gain = arrived[0, :, HALF]
    mean_square = jnp.sum(rows * rows, axis=(1, 3), keepdims=True) / D
    normed = (rows * lax.rsqrt(mean_square + epsilon) * all_gain[None, :, None, :]).astype(
        jnp.bfloat16
    )
    piece = jnp.transpose(normed, (0, 2, 1, 3)).reshape(CAP, exp_count * width)

    all_rows = lax.all_gather(piece, "z", axis=0, tiled=True)

    gates = [gate_own, swap(gate_own, "k")]
    uppers = [w_up[0], up_side, swap(w_up[0], "k"), swap(up_side, "k")]
    hidden = gate_up(place, all_rows, gates, uppers)
    hidden = lax.all_gather(hidden, ("yp", "ya"))
    out = down(place, hidden, down_own, swap(down_own, "k"))

    columns = out.shape[2]
    back = out.reshape(2, z_count, 2, HALF, columns)
    back = jnp.transpose(back, (2, 0, 1, 3, 4)).reshape(ctx_count, HALF, columns)
    back = lax.all_to_all(back, CTX, 0, 0, tiled=True)
    back = back.reshape(ctx_count // z_count, z_count, HALF, columns).astype(jnp.float32)
    summed = jnp.sum(back, axis=1).astype(jnp.bfloat16)
    summed = summed.reshape(ctx_count // z_count, HALF, columns // width, width)
    summed = jnp.transpose(summed, (0, 2, 1, 3)).reshape(exp_count, HALF, width)
    summed = jnp.pad(summed, ((0, 0), (0, PAD - HALF), (0, 0)))
    returned = lax.all_to_all(summed, EXP, 0, 0, tiled=True).reshape(table_rows, width)
    mix = jnp.where(rows_of[:, 0:1] == row_id[None, :], gate_weights[:, 0:1], 0.0) + jnp.where(
        rows_of[:, 1:2] == row_id[None, :], gate_weights[:, 1:2], 0.0
    )
    routed = jnp.dot(mix, returned.astype(jnp.float32), precision=lax.Precision.HIGHEST)
    return (stream.astype(jnp.float32) + routed).astype(jnp.bfloat16)


def solution(mesh):
    split = Mesh(
        mesh.devices.reshape(2, 2, 8, 4, 2, 2), ("yp", "ya", "z", "x", "h", "k")
    )
    return jax.shard_map(
        shards,
        mesh=split,
        in_specs=(
            P(CTX, EXP),
            P(CTX, None),
            P(CTX, None),
            P(CTX, EXP),
            P(EXP),
            P(),
            P(CTX, None),
            P(EXP, None, CTX),
            P(EXP, None, CTX),
            P(EXP, None, CTX),
        ),
        out_specs=P(CTX, EXP),
        check_vma=False,
    )
```

```python
import math

import jax
import jax.numpy as jnp
from jax import lax
from jax.experimental import pallas as pl
from jax.experimental.pallas import tpu as pltpu
from jax.sharding import Mesh, PartitionSpec as P

D = 4096
HEADS = 32
KV_HEADS = 8
HEAD_DIM = 128
EXPERTS = 8
CAP = 24
HALF = CAP // 2
PAD = 16

epsilon = 1e-05
masked_score = -1e30

CTX = ("yp", "ya", "z")
EXP = ("x", "h", "k")
SWAP = [(0, 1), (1, 0)]


def swap(value, axis):
    return lax.ppermute(value, axis, SWAP)


def slot_rows(routing):
    tokens, top = routing.shape
    flat = routing.reshape(-1)
    hits = (flat[:, None] == jnp.arange(EXPERTS, dtype=jnp.int32)[None, :]).astype(jnp.bfloat16)
    count = tokens * top
    order = jnp.arange(count, dtype=jnp.int32)
    earlier = (order[:, None] > order[None, :]).astype(jnp.bfloat16)
    before = jnp.dot(earlier, hits, preferred_element_type=jnp.float32)
    slots = jnp.sum(before * hits.astype(jnp.float32), axis=1).astype(jnp.int32)
    rows = flat * (2 * PAD) + jnp.where(slots >= HALF, slots - HALF + PAD, slots)
    return rows.reshape(tokens, top)


def attention(queries, keys, values, first):
    rows = queries.shape[0]
    heads = queries.shape[1] // HEAD_DIM
    query = jnp.transpose(queries.reshape(rows, heads, HEAD_DIM), (1, 0, 2)).reshape(
        heads * rows, HEAD_DIM
    )
    scores = lax.dot_general(
        query, keys, (((1,), (1,)), ((), ())), preferred_element_type=jnp.float32
    ) * (1.0 / math.sqrt(HEAD_DIM))
    count = keys.shape[0]
    positions = first + jnp.arange(heads * rows, dtype=jnp.int32) % rows
    visible = positions[:, None] >= jnp.arange(count, dtype=jnp.int32)[None, :]
    scores = jnp.where(visible, scores, masked_score)
    highest = jnp.max(scores, axis=1, keepdims=True)
    weights = jnp.where(visible, jnp.exp(scores - highest), 0.0)
    total = jnp.sum(weights, axis=1, keepdims=True)
    summed = jnp.dot(weights.astype(jnp.bfloat16), values, preferred_element_type=jnp.float32)
    out = (summed / total).reshape(heads, rows, HEAD_DIM)
    return jnp.transpose(out, (1, 0, 2)).reshape(rows, heads * HEAD_DIM).astype(jnp.bfloat16)


def gate_up_kernel(place, rows, gate_own, gate_far, *refs):
    uppers, out, total = refs[0:4], refs[4], refs[5]
    step = pl.program_id(0)
    columns = [gate_own[0], gate_own[1], gate_far[0], gate_far[1]] + [ref[...] for ref in uppers]
    product = jnp.dot(
        rows[...], jnp.concatenate(columns, axis=1), preferred_element_type=jnp.float32
    )

    @pl.when(step == 0)
    def _():
        total[...] = product

    @pl.when(step != 0)
    def _():
        total[...] += product

    @pl.when(step == pl.num_programs(0) - 1)
    def _():
        unit = gate_own.shape[2]
        first = place[1] == 0
        for part in range(2):
            mine = total[:, (4 + 2 * part) * unit : (5 + 2 * part) * unit]
            side = total[:, (5 + 2 * part) * unit : (6 + 2 * part) * unit]
            for half in range(2):
                at = 2 * part + half
                gate = total[:, at * unit : (at + 1) * unit]
                upper = jnp.where(first, mine, side) if half == 0 else jnp.where(first, side, mine)
                hidden = gate / (1.0 + jnp.exp(-gate)) * upper
                out[:, at * unit : (at + 1) * unit] = hidden.astype(jnp.bfloat16)


def gate_up(place, rows, gates, uppers):
    count, depth = rows.shape
    unit = uppers[0].shape[1]
    chunk = 2048
    return pl.pallas_call(
        gate_up_kernel,
        out_shape=jax.ShapeDtypeStruct((count, 4 * unit), jnp.bfloat16),
        grid_spec=pltpu.PrefetchScalarGridSpec(
            num_scalar_prefetch=1,
            grid=(depth // chunk,),
            in_specs=[pl.BlockSpec((count, chunk), lambda i, place: (0, i))]
            + [pl.BlockSpec((2, chunk, unit), lambda i, place: (0, i, 0))] * 2
            + [pl.BlockSpec((chunk, unit), lambda i, place: (i, 0))] * 4,
            out_specs=pl.BlockSpec((count, 4 * unit), lambda i, place: (0, 0)),
            scratch_shapes=[pltpu.VMEM((count, 8 * unit), jnp.float32)],
        ),
        compiler_params=pltpu.CompilerParams(vmem_limit_bytes=60 * 1024 * 1024),
        cost_estimate=pl.CostEstimate(
            flops=2 * count * depth * 8 * unit,
            bytes_accessed=2 * depth * (count + 8 * unit),
            transcendentals=count * 4 * unit,
        ),
    )(place, rows, *gates, *uppers)


def down_kernel(hidden, own, far, out, product, sorted_rows):
    rows = hidden.shape[1]
    groups, _, unit = own.shape
    blocks = out.shape[0] // 4
    parts = []
    for part in range(2):
        at = slice(2 * part * unit, (2 * part + 2) * unit)
        wide = [
            jnp.concatenate([hidden[parity, :, at], hidden[2 + parity, :, at]], axis=1)
            for parity in range(2)
        ]
        parts.append(jnp.concatenate(wide, axis=0))
    for pair in range(0, groups, 2):
        total = None
        for part, weights in enumerate((own, far)):
            columns = jnp.concatenate([weights[pair], weights[pair + 1]], axis=1)
            term = jnp.dot(parts[part], columns, preferred_element_type=jnp.float32)
            total = term if total is None else total + term
        product[...] = total
        for which in range(2):
            lanes = slice(which * unit, (which + 1) * unit)
            to = (pair + which) * HALF
            for parity in range(2):
                for z in range(blocks):
                    at = parity * rows + z * CAP
                    near, distant = parity * blocks + z, (2 + parity) * blocks + z
                    sorted_rows[near, to : to + HALF] = product[at : at + HALF, lanes]
                    sorted_rows[distant, to : to + HALF] = product[at + HALF : at + CAP, lanes]
    out[...] = sorted_rows[...].astype(jnp.bfloat16)


def down(hidden, own, far, blocks):
    count = hidden.shape[1]
    groups, depth, unit = own.shape
    whole = lambda array: pl.BlockSpec(array.shape, lambda i: (0,) * len(array.shape))
    result = jax.ShapeDtypeStruct((blocks, groups * HALF, unit), jnp.bfloat16)
    return pl.pallas_call(
        down_kernel,
        out_shape=result,
        grid=(1,),
        in_specs=[whole(hidden), whole(own), whole(far)],
        out_specs=whole(result),
        scratch_shapes=[
            pltpu.VMEM((2 * count, 2 * unit), jnp.float32),
            pltpu.VMEM(result.shape, jnp.float32),
        ],
        compiler_params=pltpu.CompilerParams(vmem_limit_bytes=32 * 1024 * 1024),
        cost_estimate=pl.CostEstimate(
            flops=2 * 2 * count * 2 * depth * groups * unit,
            bytes_accessed=2 * (hidden.size + 2 * own.size + 2 * count * groups * unit),
            transcendentals=0,
        ),
    )(hidden, own, far)


def shards(queries, keys, values, residual, gain, expert_ids, gate_weights, w_gate, w_up, w_down):
    seq_rows = queries.shape[0]
    width = queries.shape[1]
    z_count = lax.axis_size("z")
    ctx_count = lax.axis_size(CTX)
    exp_count = lax.axis_size(EXP)
    ctx_index = lax.axis_index(CTX)
    core = lax.axis_index("k")
    place = jnp.stack([lax.axis_index("yp"), lax.axis_index("ya")]).astype(jnp.int32)

    head = (lax.axis_index("x") * 2 + lax.axis_index("h")) * HEAD_DIM
    key_part = lax.dynamic_slice_in_dim(keys, head, HEAD_DIM, 1)
    value_part = lax.dynamic_slice_in_dim(values, head, HEAD_DIM, 1)
    sent = jnp.where(core == 0, key_part, value_part)
    gate_own = lax.all_gather(w_gate[0], "ya")
    held = lax.all_to_all(
        jnp.broadcast_to(sent[None], (ctx_count, seq_rows, HEAD_DIM)), CTX, 0, 0, tiled=True
    ).reshape(ctx_count * seq_rows, HEAD_DIM)
    w_up, w_down, held = lax.optimization_barrier((w_up, w_down, held))
    up_side = swap(w_up[0], "ya")
    far = swap(held, "k")
    all_keys = jnp.where(core == 0, held, far)
    all_values = jnp.where(core == 0, far, held)

    unit = w_down.shape[2]
    cut = w_down[0].reshape(ctx_count // z_count, z_count, unit, unit)
    cut = jnp.transpose(cut, (1, 0, 2, 3)).reshape(z_count, ctx_count // z_count * unit, unit)

    heads = attention(queries, all_keys, all_values, ctx_index * seq_rows)
    stream = (residual.astype(jnp.float32) + heads.astype(jnp.float32)).astype(jnp.bfloat16)

    block_ids = lax.dynamic_slice_in_dim(expert_ids, ctx_index * seq_rows, seq_rows, 0)
    rows_of = slot_rows(block_ids)
    table_rows = EXPERTS * 2 * PAD
    row_id = jnp.arange(table_rows, dtype=jnp.int32)
    taken = (row_id[:, None] == rows_of[None, :, 0]) | (row_id[:, None] == rows_of[None, :, 1])
    gain_row = ((row_id % PAD) == HALF)[:, None]
    table = jnp.concatenate(
        [taken, gain_row, jnp.zeros((table_rows, 15), jnp.bool_)], axis=1
    ).astype(jnp.bfloat16)
    source = jnp.concatenate(
        [stream, gain[None, :], jnp.zeros((15, width), jnp.bfloat16)], axis=0
    )
    outgoing = jnp.dot(table, source, preferred_element_type=jnp.float32).astype(jnp.bfloat16)
    outgoing = jnp.broadcast_to(
        outgoing.reshape(1, exp_count, PAD, width), (2, exp_count, PAD, width)
    ).reshape(2 * exp_count, PAD, width)
    arrived = lax.all_to_all(outgoing, ("yp",) + EXP, 0, 0, tiled=True)
    arrived = arrived.reshape(2, exp_count, PAD, width).astype(jnp.float32)
    rows = arrived[:, :, :HALF]
    all_gain = arrived[0, :, HALF]
    mean_square = jnp.sum(rows * rows, axis=(1, 3), keepdims=True) / D
    normed = (rows * lax.rsqrt(mean_square + epsilon) * all_gain[None, :, None, :]).astype(
        jnp.bfloat16
    )
    piece = jnp.transpose(normed, (0, 2, 1, 3)).reshape(CAP, exp_count * width)

    all_rows = lax.all_gather(piece, "z", axis=0, tiled=True)
    gates = [gate_own, swap(gate_own, "k")]
    uppers = [w_up[0], up_side, swap(w_up[0], "k"), swap(up_side, "k")]
    down_own = lax.all_to_all(cut, "z", 0, 0, tiled=True)
    hidden = gate_up(place, all_rows, gates, uppers)
    hidden = lax.all_gather(hidden, ("yp", "ya"))
    back = down(hidden, down_own, swap(down_own, "k"), ctx_count)
    back = lax.all_to_all(back, CTX, 0, 0, tiled=True)
    back = back.reshape(ctx_count // z_count, z_count, z_count * HALF, unit).astype(jnp.float32)
    summed = jnp.sum(back, axis=1).astype(jnp.bfloat16)
    tall = width // unit * HALF
    returned = lax.all_to_all(summed.reshape(exp_count, tall, unit), EXP, 0, 0, tiled=True)
    returned = returned.reshape(exp_count * tall, unit).astype(jnp.float32)
    place_of = rows_of // PAD * tall + rows_of % PAD
    order = jnp.arange(exp_count * tall, dtype=jnp.int32)
    mixes = []
    for column in range(width // unit):
        at = place_of + column * HALF
        mixes.append(
            jnp.where(at[:, 0:1] == order[None, :], gate_weights[:, 0:1], 0.0)
            + jnp.where(at[:, 1:2] == order[None, :], gate_weights[:, 1:2], 0.0)
        )
    routed = jnp.dot(jnp.concatenate(mixes, axis=0), returned, precision=lax.Precision.HIGHEST)
    routed = jnp.concatenate(
        [routed[i * seq_rows : (i + 1) * seq_rows] for i in range(len(mixes))], axis=1
    )
    return (stream.astype(jnp.float32) + routed).astype(jnp.bfloat16)


def solution(mesh):
    split = Mesh(
        mesh.devices.reshape(2, 2, 8, 4, 2, 2), ("yp", "ya", "z", "x", "h", "k")
    )
    return jax.shard_map(
        shards,
        mesh=split,
        in_specs=(
            P(CTX, EXP),
            P(CTX, None),
            P(CTX, None),
            P(CTX, EXP),
            P(EXP),
            P(),
            P(CTX, None),
            P(EXP, None, CTX),
            P(EXP, None, CTX),
            P(EXP, None, CTX),
        ),
        out_specs=P(CTX, EXP),
        check_vma=False,
    )
```

```python
import math

import jax
import jax.numpy as jnp
from jax import lax
from jax.experimental import pallas as pl
from jax.experimental.pallas import tpu as pltpu
from jax.sharding import Mesh, PartitionSpec as P

D = 4096
HEADS = 32
KV_HEADS = 8
HEAD_DIM = 128
EXPERTS = 8
CAP = 24
HALF = CAP // 2
PAD = 16

epsilon = 1e-05
masked_score = -1e30

CTX = ("yp", "ya", "z")
EXP = ("x", "h", "k")
SWAP = [(0, 1), (1, 0)]


def swap(value, axis):
    return lax.ppermute(value, axis, SWAP)


def slot_rows(routing):
    tokens, top = routing.shape
    flat = routing.reshape(-1)
    hits = (flat[:, None] == jnp.arange(EXPERTS, dtype=jnp.int32)[None, :]).astype(jnp.bfloat16)
    count = tokens * top
    order = jnp.arange(count, dtype=jnp.int32)
    earlier = (order[:, None] > order[None, :]).astype(jnp.bfloat16)
    before = jnp.dot(earlier, hits, preferred_element_type=jnp.float32)
    slots = jnp.sum(before * hits.astype(jnp.float32), axis=1).astype(jnp.int32)
    rows = flat * (2 * PAD) + jnp.where(slots >= HALF, slots - HALF + PAD, slots)
    return rows.reshape(tokens, top)


def attention(queries, keys, values, first):
    rows = queries.shape[0]
    heads = queries.shape[1] // HEAD_DIM
    query = jnp.transpose(queries.reshape(rows, heads, HEAD_DIM), (1, 0, 2)).reshape(
        heads * rows, HEAD_DIM
    )
    scores = lax.dot_general(
        query, keys, (((1,), (1,)), ((), ())), preferred_element_type=jnp.float32
    ) * (1.0 / math.sqrt(HEAD_DIM))
    count = keys.shape[0]
    positions = first + jnp.arange(heads * rows, dtype=jnp.int32) % rows
    visible = positions[:, None] >= jnp.arange(count, dtype=jnp.int32)[None, :]
    scores = jnp.where(visible, scores, masked_score)
    highest = jnp.max(scores, axis=1, keepdims=True)
    weights = jnp.where(visible, jnp.exp(scores - highest), 0.0)
    total = jnp.sum(weights, axis=1, keepdims=True)
    summed = jnp.dot(weights.astype(jnp.bfloat16), values, preferred_element_type=jnp.float32)
    out = (summed / total).reshape(heads, rows, HEAD_DIM)
    return jnp.transpose(out, (1, 0, 2)).reshape(rows, heads * HEAD_DIM).astype(jnp.bfloat16)


def gate_up_kernel(place, rows, gate_own, gate_far, *refs):
    sides, uppers, out, total = (refs[0:2], refs[2:4]), refs[4:8], refs[8], refs[9]
    step = pl.program_id(0)

    def product(side, side_far):
        columns = [ref[...] for ref in (gate_own, side, gate_far, side_far, *uppers)]
        return jnp.dot(
            rows[...], jnp.concatenate(columns, axis=1), preferred_element_type=jnp.float32
        )

    @pl.when(step == 0)
    def _():
        total[...] = product(*sides[0])

    @pl.when(step == 1)
    def _():
        total[...] += product(*sides[1])
        width = out.shape[1]
        unit = width // 4
        first = place[1] == 0
        for part in range(2):
            pair = []
            for half in range(2):
                at = (2 * part + half) * unit
                gate = total[:, at : at + unit]
                upper = total[:, width + at : width + at + unit]
                pair.append((gate / (1.0 + jnp.exp(-gate)) * upper).astype(jnp.bfloat16))
            at = 2 * part * unit
            out[:, at : at + unit] = jnp.where(first, pair[0], pair[1])
            out[:, at + unit : at + 2 * unit] = jnp.where(first, pair[1], pair[0])


def gate_up(place, rows, gates, sides, uppers):
    count, depth = rows.shape
    unit = uppers[0].shape[1]
    chunk = depth // 2
    by_step = pl.BlockSpec((chunk, unit), lambda i, place: (i, 0))
    fixed = pl.BlockSpec((chunk, unit), lambda i, place: (0, 0))
    return pl.pallas_call(
        gate_up_kernel,
        out_shape=jax.ShapeDtypeStruct((count, 4 * unit), jnp.bfloat16),
        grid_spec=pltpu.PrefetchScalarGridSpec(
            num_scalar_prefetch=1,
            grid=(2,),
            in_specs=[pl.BlockSpec((count, chunk), lambda i, place: (0, i))]
            + [by_step] * 2
            + [fixed] * 4
            + [by_step] * 4,
            out_specs=pl.BlockSpec((count, 4 * unit), lambda i, place: (0, 0)),
            scratch_shapes=[pltpu.VMEM((count, 8 * unit), jnp.float32)],
        ),
        compiler_params=pltpu.CompilerParams(vmem_limit_bytes=60 * 1024 * 1024),
        cost_estimate=pl.CostEstimate(
            flops=2 * count * depth * 8 * unit,
            bytes_accessed=2 * depth * (count + 8 * unit),
            transcendentals=count * 4 * unit,
        ),
    )(place, rows, *gates, *sides, *uppers)


def down_kernel(hidden, own, far, out, product, sorted_rows):
    rows = hidden.shape[1]
    groups, _, unit = own.shape
    blocks = out.shape[0] // 4
    parts = []
    for part in range(2):
        at = slice(2 * part * unit, (2 * part + 2) * unit)
        wide = [
            jnp.concatenate([hidden[parity, :, at], hidden[2 + parity, :, at]], axis=1)
            for parity in range(2)
        ]
        parts.append(jnp.concatenate(wide, axis=0))
    for pair in range(0, groups, 2):
        total = None
        for part, weights in enumerate((own, far)):
            columns = jnp.concatenate([weights[pair], weights[pair + 1]], axis=1)
            term = jnp.dot(parts[part], columns, preferred_element_type=jnp.float32)
            total = term if total is None else total + term
        product[...] = total
        for which in range(2):
            lanes = slice(which * unit, (which + 1) * unit)
            to = (pair + which) * HALF
            for parity in range(2):
                for z in range(blocks):
                    at = parity * rows + z * CAP
                    near, distant = parity * blocks + z, (2 + parity) * blocks + z
                    sorted_rows[near, to : to + HALF] = product[at : at + HALF, lanes]
                    sorted_rows[distant, to : to + HALF] = product[at + HALF : at + CAP, lanes]
    out[...] = sorted_rows[...].astype(jnp.bfloat16)


def down(hidden, own, far, blocks):
    count = hidden.shape[1]
    groups, depth, unit = own.shape
    whole = lambda array: pl.BlockSpec(array.shape, lambda i: (0,) * len(array.shape))
    result = jax.ShapeDtypeStruct((blocks, groups * HALF, unit), jnp.bfloat16)
    return pl.pallas_call(
        down_kernel,
        out_shape=result,
        grid=(1,),
        in_specs=[whole(hidden), whole(own), whole(far)],
        out_specs=whole(result),
        scratch_shapes=[
            pltpu.VMEM((2 * count, 2 * unit), jnp.float32),
            pltpu.VMEM(result.shape, jnp.float32),
        ],
        compiler_params=pltpu.CompilerParams(vmem_limit_bytes=32 * 1024 * 1024),
        cost_estimate=pl.CostEstimate(
            flops=2 * 2 * count * 2 * depth * groups * unit,
            bytes_accessed=2 * (hidden.size + 2 * own.size + 2 * count * groups * unit),
            transcendentals=0,
        ),
    )(hidden, own, far)


def shards(queries, keys, values, residual, gain, expert_ids, gate_weights, w_gate, w_up, w_down):
    seq_rows = queries.shape[0]
    width = queries.shape[1]
    z_count = lax.axis_size("z")
    ctx_count = lax.axis_size(CTX)
    exp_count = lax.axis_size(EXP)
    ctx_index = lax.axis_index(CTX)
    core = lax.axis_index("k")
    place = jnp.stack([lax.axis_index("yp"), lax.axis_index("ya")]).astype(jnp.int32)

    head = (lax.axis_index("x") * 2 + lax.axis_index("h")) * HEAD_DIM
    key_part = lax.dynamic_slice_in_dim(keys, head, HEAD_DIM, 1)
    value_part = lax.dynamic_slice_in_dim(values, head, HEAD_DIM, 1)
    sent = jnp.where(core == 0, key_part, value_part)
    middle = w_gate.shape[1] // 2
    held = lax.all_to_all(
        jnp.broadcast_to(sent[None], (ctx_count, seq_rows, HEAD_DIM)), CTX, 0, 0, tiled=True
    ).reshape(ctx_count * seq_rows, HEAD_DIM)
    low_own, high_own = w_gate[0, :middle], w_gate[0, middle:]
    w_up, w_down, held, low_own, high_own = lax.optimization_barrier(
        (w_up, w_down, held, low_own, high_own)
    )
    up_side = swap(w_up[0], "ya")
    far = swap(held, "k")
    all_keys = jnp.where(core == 0, held, far)
    all_values = jnp.where(core == 0, far, held)

    unit = w_down.shape[2]
    cut = w_down[0].reshape(ctx_count // z_count, z_count, unit, unit)
    cut = jnp.transpose(cut, (1, 0, 2, 3)).reshape(z_count, ctx_count // z_count * unit, unit)

    heads = attention(queries, all_keys, all_values, ctx_index * seq_rows)
    stream = (residual.astype(jnp.float32) + heads.astype(jnp.float32)).astype(jnp.bfloat16)

    block_ids = lax.dynamic_slice_in_dim(expert_ids, ctx_index * seq_rows, seq_rows, 0)
    rows_of = slot_rows(block_ids)
    table_rows = EXPERTS * 2 * PAD
    row_id = jnp.arange(table_rows, dtype=jnp.int32)
    taken = (row_id[:, None] == rows_of[None, :, 0]) | (row_id[:, None] == rows_of[None, :, 1])
    gain_row = ((row_id % PAD) == HALF)[:, None]
    table = jnp.concatenate(
        [taken, gain_row, jnp.zeros((table_rows, 15), jnp.bool_)], axis=1
    ).astype(jnp.bfloat16)
    source = jnp.concatenate(
        [stream, gain[None, :], jnp.zeros((15, width), jnp.bfloat16)], axis=0
    )
    outgoing = jnp.dot(table, source, preferred_element_type=jnp.float32).astype(jnp.bfloat16)
    low_side = swap(low_own, "ya")
    outgoing = jnp.broadcast_to(
        outgoing.reshape(1, exp_count, PAD, width), (2, exp_count, PAD, width)
    ).reshape(2 * exp_count, PAD, width)
    arrived = lax.all_to_all(outgoing, ("yp",) + EXP, 0, 0, tiled=True)
    arrived, low_side, cut = lax.optimization_barrier((arrived, low_side, cut))
    high_side = swap(high_own, "ya")
    arrived = arrived.reshape(2, exp_count, PAD, width).astype(jnp.float32)
    rows = arrived[:, :, :HALF]
    all_gain = arrived[0, :, HALF]
    mean_square = jnp.sum(rows * rows, axis=(1, 3), keepdims=True) / D
    normed = (rows * lax.rsqrt(mean_square + epsilon) * all_gain[None, :, None, :]).astype(
        jnp.bfloat16
    )
    piece = jnp.transpose(normed, (0, 2, 1, 3)).reshape(CAP, exp_count * width)

    all_rows = lax.all_to_all(
        jnp.broadcast_to(piece[None], (z_count,) + piece.shape), "z", 0, 0, tiled=True
    ).reshape(z_count * CAP, piece.shape[1])
    gate_far, up_far, low_side_far = swap(w_gate[0], "k"), swap(w_up[0], "k"), swap(low_side, "k")
    high_side, up_side, gate_far, up_far, low_side_far = lax.optimization_barrier(
        (high_side, up_side, gate_far, up_far, low_side_far)
    )
    gates = [w_gate[0], gate_far]
    sides = [low_side, low_side_far, high_side, swap(high_side, "k")]
    uppers = [w_up[0], up_side, up_far, swap(up_side, "k")]
    all_rows, cut = lax.optimization_barrier((all_rows, cut))
    down_own = lax.all_to_all(cut, "z", 0, 0, tiled=True)
    hidden = gate_up(place, all_rows, gates, sides, uppers)
    hidden = lax.all_gather(hidden, ("yp", "ya"))
    hidden, down_own = lax.optimization_barrier((hidden, down_own))
    back = down(hidden, down_own, swap(down_own, "k"), ctx_count)
    back = lax.all_to_all(back, CTX, 0, 0, tiled=True)
    back = back.reshape(ctx_count // z_count, z_count, z_count * HALF, unit).astype(jnp.float32)
    summed = jnp.sum(back, axis=1).astype(jnp.bfloat16)
    tall = width // unit * HALF
    returned = lax.all_to_all(summed.reshape(exp_count, tall, unit), EXP, 0, 0, tiled=True)
    returned = returned.reshape(exp_count * tall, unit).astype(jnp.float32)
    place_of = rows_of // PAD * tall + rows_of % PAD
    order = jnp.arange(exp_count * tall, dtype=jnp.int32)
    mixes = []
    for column in range(width // unit):
        at = place_of + column * HALF
        mixes.append(
            jnp.where(at[:, 0:1] == order[None, :], gate_weights[:, 0:1], 0.0)
            + jnp.where(at[:, 1:2] == order[None, :], gate_weights[:, 1:2], 0.0)
        )
    routed = jnp.dot(jnp.concatenate(mixes, axis=0), returned, precision=lax.Precision.HIGHEST)
    routed = jnp.concatenate(
        [routed[i * seq_rows : (i + 1) * seq_rows] for i in range(len(mixes))], axis=1
    )
    return (stream.astype(jnp.float32) + routed).astype(jnp.bfloat16)


def solution(mesh):
    split = Mesh(
        mesh.devices.reshape(2, 2, 8, 4, 2, 2), ("yp", "ya", "z", "x", "h", "k")
    )
    return jax.shard_map(
        shards,
        mesh=split,
        in_specs=(
            P(CTX, EXP),
            P(CTX, None),
            P(CTX, None),
            P(CTX, EXP),
            P(EXP),
            P(),
            P(CTX, None),
            P(EXP, None, CTX),
            P(EXP, None, CTX),
            P(EXP, None, CTX),
        ),
        out_specs=P(CTX, EXP),
        check_vma=False,
    )
```
